32 devices in a mesh: section: 8 (over z, y), dp: 4 (over x, core).
Axes of the slice: x: 2, y: 2, z: 4, core: 2. Of those that a mesh axis runs over, the one named last changes fastest.
Arguments:
- initial_block_entries: bfloat16 [4, 8, 144, 5120], P('dp', 'section'), may hold values from -6 to 6
- incoming_tokens: bfloat16 [4, 3, 128, 5120], P('dp', None, None, 'section'), may hold values from -6 to 6
- adjoint_flow: bfloat16 [4, 8, 4, 144, 5120], P('dp', 'section'), may hold values from -6 to 6
- address_projector: bfloat16 [8, 5120, 128], P('section', 'dp'), may hold values from -0.078125 to 0.078125
- rescale_factor: bfloat16 [8, 5120], P('section'), may hold values from 0.5 to 1.5
- storage_rate_projector: bfloat16 [8, 5120], P('section'), may hold values from -0.078125 to 0.078125
- associative_store: float32 [4, 8, 128, 5120], P('dp', 'section'), may hold values from -480 to 480
- recall_scaling: float32 [4, 8, 128], P('dp', 'section'), may hold values from 4 to 40
Outputs:
- final_tick_outcomes: bfloat16 [4, 8, 144, 5120], P('dp', 'section')
- address_derivative: float32 [8, 5120, 128], P('section', 'dp')
The draws below stay inside these ranges and needn't reach their ends.
All inputs are finite; a program needn't handle non-finite values.
Results may differ from the reference program's by a relative error of at most 0.0061.
Values may be sent and summed in bfloat16 or wider, within the bound.
A program may use at most 128 MiB of HBM per device.

```python
import math
import jax
import jax.numpy as jnp
from jax import lax

EMBED_SPAN = 5120
DK = 128
SEG = 128
TICKS = 4
PASSAGE_LINES = 144
DEPTH_PARTS = 8
CORPUS_TEXTS = 4


def shard_levels(rng, shape, pieces, least, top_value):
    gain = 1.0
    for position, shards_of in pieces:
        steps = jax.random.uniform(jax.random.fold_in(jax.random.fold_in(rng, 6), position), (shards_of,), jnp.float32, least / len(pieces), top_value / len(pieces))
        gain = gain * jnp.repeat(jnp.exp(steps), shape[position] // shards_of).reshape((-1,) + (1,) * (len(shape) - 1 - position))
    return gain


def noise(own_key, extent, deviation, reach, shards=(), dtype=jnp.bfloat16):
    values = deviation * jax.random.normal(own_key, extent, jnp.float32)
    if shards:
        values = values * shard_levels(own_key, extent, shards, -0.22, 0.18)
    return jnp.clip(values, -reach, reach).astype(dtype)


def setup_inputs(seed: int = 0) -> dict:
    seeds = jax.random.split(jax.random.key(seed), 9)
    return {
        "initial_block_entries": noise(seeds[0], (CORPUS_TEXTS, DEPTH_PARTS, PASSAGE_LINES, EMBED_SPAN), 1.0, 6.0, ((0, 4), (1, 8))),
        "incoming_tokens": noise(seeds[1], (CORPUS_TEXTS, TICKS - 1, SEG, EMBED_SPAN), 1.0, 6.0, ((0, 4), (3, 8))),
        "adjoint_flow": noise(seeds[2], (CORPUS_TEXTS, DEPTH_PARTS, TICKS, PASSAGE_LINES, EMBED_SPAN), 1.0, 6.0, ((0, 4), (1, 8))),
        "address_projector": noise(seeds[3], (DEPTH_PARTS, EMBED_SPAN, DK), EMBED_SPAN ** -0.5, 0.078125, ((0, 8), (1, 4))),
        "rescale_factor": jnp.clip(1.0 + 0.1 * jax.random.normal(seeds[4], (DEPTH_PARTS, EMBED_SPAN), jnp.float32), 0.5, 1.5).astype(jnp.bfloat16),
        "storage_rate_projector": noise(seeds[5], (DEPTH_PARTS, EMBED_SPAN), EMBED_SPAN ** -0.5, 0.078125, ((0, 8),)),
        "associative_store": noise(seeds[6], (CORPUS_TEXTS, DEPTH_PARTS, DK, EMBED_SPAN), 80.0, 480.0, ((0, 4), (1, 8)), jnp.float32),
        "recall_scaling": jnp.clip(jnp.exp(math.log(40.0) - 2.3025851 * jax.random.uniform(seeds[7], (CORPUS_TEXTS, DEPTH_PARTS, DK), jnp.float32) ** shard_levels(seeds[7], (CORPUS_TEXTS, DEPTH_PARTS, DK), ((0, 4), (1, 8)), -0.2, 0.2)), 4.0, 40.0),
    }


HIGH = lax.Precision.HIGHEST

def one_doc(gradsum, item_list, address_projector, rescale_factor, storage_rate_projector):
    awaiting_breadth_size, fresh_width, cotangent_width, value_rows, norm_values = item_list
    weights = address_projector.astype(jnp.float32)
    gains = rescale_factor.astype(jnp.float32)
    betas = storage_rate_projector.astype(jnp.float32)
    recurrent_vector = awaiting_breadth_size
    produced_entries = awaiting_breadth_size
    for tick in range(TICKS):
        if tick > 0:
            cycled_array = jnp.roll(produced_entries, 1, axis=0)
            attention_channel = jnp.concatenate([fresh_width[tick - 1], produced_entries[-1, SEG:]], axis=0)
            recurrent_vector = cycled_array.at[0].set(attention_channel)
        channel_features = recurrent_vector.astype(jnp.float32)
        meansq = lax.optimization_barrier(jnp.mean(channel_features * channel_features, axis=-1, keepdims=True))
        normed = (channel_features * lax.rsqrt(meansq + 1e-06) * gains[:, None, :]).astype(jnp.bfloat16)
        nf = normed.astype(jnp.float32)
        pre = jnp.einsum('srd,sdk->srk', nf, weights)
        query = jax.nn.elu(pre) + 1.0
        num = jnp.einsum('srk,skd->srd', query, value_rows, precision=HIGH)
        den = 1.0 + jnp.einsum('srk,sk->sr', query, norm_values, precision=HIGH)
        produced_entries = (channel_features + num / den[..., None]).astype(jnp.bfloat16)
        grad_out = cotangent_width[:, tick].astype(jnp.float32)
        dnum = grad_out / den[..., None]
        dden = -lax.optimization_barrier(jnp.sum(grad_out * num, axis=-1)) / (den * den)
        dq = jnp.einsum('srd,skd->srk', dnum, value_rows, precision=HIGH) + dden[..., None] * norm_values[:, None, :]
        slope = jnp.where(pre > 0, 1.0, jnp.exp(jnp.minimum(pre, 0.0)))
        key_cot = (dq * slope).astype(jnp.bfloat16).astype(jnp.float32)
        gradsum = gradsum + jnp.einsum('srd,srk->sdk', nf, key_cot)
        mem_keys = query[:, SEG:]
        mem_vals = nf[:, SEG:]
        beta = jax.nn.sigmoid(jnp.einsum('srd,sd->sr', mem_vals, betas))
        prev = jnp.einsum('srk,skd->srd', mem_keys, value_rows, precision=HIGH)
        prev = prev / (1.0 + jnp.einsum('srk,sk->sr', mem_keys, norm_values, precision=HIGH))[..., None]
        value_rows = value_rows + jnp.einsum('srk,srd->skd', mem_keys, beta[..., None] * (mem_vals - prev), precision=HIGH)
        norm_values = norm_values + jnp.einsum('srk,sr->sk', mem_keys, beta, precision=HIGH)
    return (gradsum, produced_entries)

def reference(initial_block_entries, incoming_tokens, adjoint_flow, address_projector, rescale_factor, storage_rate_projector, associative_store, recall_scaling):
    opening_offset = jnp.zeros((DEPTH_PARTS, EMBED_SPAN, DK), jnp.float32)

    def iteration_number(carry, item_list):
        return one_doc(carry, item_list, address_projector, rescale_factor, storage_rate_projector)
    address_derivative, final_tick_outcomes = lax.scan(iteration_number, opening_offset, (initial_block_entries, incoming_tokens, adjoint_flow, associative_store, recall_scaling))
    return (final_tick_outcomes, address_derivative)
```

```python
import functools

import jax
import jax.numpy as jnp
from jax import lax
from jax.experimental import pallas as pl
from jax.experimental.pallas import tpu as pltpu
from jax.sharding import PartitionSpec as P

HIGH = lax.Precision.HIGHEST


def from_behind(array, axis, by):
    peers = lax.axis_size(axis)
    return lax.ppermute(array, axis, [(i, (i + by) % peers) for i in range(peers)])


def per_device(
    initial_block_entries,
    incoming_tokens,
    adjoint_flow,
    address_projector,
    rescale_factor,
    storage_rate_projector,
    associative_store,
    recall_scaling,
):
    leading_block = lax.axis_index("section") == 0
    seg_rows = incoming_tokens.shape[2]
    ticks = adjoint_flow.shape[2]
    line_breadth = initial_block_entries.shape[3]
    keysize = address_projector.shape[2]
    gain_row = rescale_factor[0].astype(jnp.float32)
    beta_col = storage_rate_projector[0]
    value_rows = associative_store[0, 0]
    norm_values = recall_scaling[0, 0]
    whole = lax.all_gather(address_projector[0], "dp", axis=0, tiled=True)
    recurrent_vector = initial_block_entries[0, 0]
    produced_entries = recurrent_vector
    local_total = jnp.zeros((line_breadth, keysize), jnp.float32)
    for tick in range(ticks):
        if tick > 0:
            columns = lax.all_gather(incoming_tokens[0, tick - 1], "section", axis=1, tiled=True)
            shifted_along = from_behind(produced_entries, "section", 1)
            loop_rows = shifted_along[seg_rows:]
            attention_channel = jnp.concatenate([columns, loop_rows], axis=0)
            recurrent_vector = jnp.where(leading_block, attention_channel, shifted_along)
        channel_features = recurrent_vector.astype(jnp.float32)
        meansq = jnp.mean(channel_features * channel_features, axis=-1, keepdims=True)
        normed = (channel_features * lax.rsqrt(meansq + 1e-06) * gain_row).astype(jnp.bfloat16)
        pre = jnp.dot(normed, whole, preferred_element_type=jnp.float32)
        query = jax.nn.elu(pre) + 1.0
        num = jnp.dot(query, value_rows, precision=HIGH)
        den = 1.0 + jnp.dot(query, norm_values, precision=HIGH)
        produced_entries = (channel_features + num / den[:, None]).astype(jnp.bfloat16)
        grad_out = adjoint_flow[0, 0, tick].astype(jnp.float32)
        dnum = grad_out / den[:, None]
        dden = -jnp.sum(grad_out * num, axis=-1) / (den * den)
        dq = (
            jnp.einsum("rd,kd->rk", dnum, value_rows, precision=HIGH)
            + dden[:, None] * norm_values[None, :]
        )
        slope = jnp.where(pre > 0, 1.0, jnp.exp(jnp.minimum(pre, 0.0)))
        key_cot = (dq * slope).astype(jnp.bfloat16)
        term = jnp.einsum("rd,rk->dk", normed, key_cot, preferred_element_type=jnp.float32)
        local_total = local_total + term
        mem_keys = query[seg_rows:]
        mem_vals = normed[seg_rows:].astype(jnp.float32)
        beta = jax.nn.sigmoid(
            jnp.dot(normed[seg_rows:], beta_col, preferred_element_type=jnp.float32)
        )
        prev = jnp.dot(mem_keys, value_rows, precision=HIGH)
        prev = prev / (1.0 + jnp.dot(mem_keys, norm_values, precision=HIGH))[:, None]
        value_rows = value_rows + jnp.einsum(
            "rk,rd->kd", mem_keys, beta[:, None] * (mem_vals - prev), precision=HIGH
        )
        norm_values = norm_values + jnp.einsum("rk,r->k", mem_keys, beta, precision=HIGH)
    summed = lax.psum_scatter(local_total, "dp", scatter_dimension=0, tiled=True)
    return (produced_entries[None, None], summed[None])


MESH = pl.DeviceIdType.MESH
NT = (((1,), (1,)), ((), ()))
TN = (((0,), (0,)), ((), ()))
F32 = jnp.float32
BF16 = jnp.bfloat16


def dot(a, b, dims=(((1,), (0,)), ((), ()))):
    return lax.dot_general(a, b, dims, preferred_element_type=F32)


def fused(
    sections, docs, ticks, seg,
    h0_any, tok_any, g_any, w_any, gain, rate, a_any, z_in,
    y_out, ad_out,
    h0, hbuf, ybuf, g, w_own, w, a32, a16, z, cot, fbuf, kbuf, adt,
    load_sem, send_w, recv_w, send_tok, recv_tok, send_y, recv_y,
    send_f, recv_f, send_k, recv_k,
):
    sec, me = lax.axis_index("section"), lax.axis_index("dp")
    rows, width = h0.shape
    mem = rows - seg
    span = width // docs
    cw = width // sections
    per = span // cw
    follower = lax.rem(sec + 1, sections)
    first, last = sec == 0, sec == sections - 1

    def peer(i):
        return lax.rem(me + i, docs)

    def cols(c, size=cw):
        return pl.ds(pl.multiple_of(c * size, 128), size)

    def remote(src, dst, send, recv, device):
        return pltpu.make_async_remote_copy(
            src_ref=src, dst_ref=dst, send_sem=send, recv_sem=recv,
            device_id=device, device_id_type=MESH,
        )

    own_w = w.at[pl.ds(pl.multiple_of(me * span, 128), span)]
    load_w = pltpu.make_async_copy(w_any.at[0], w_own, load_sem.at[0])
    load_h = pltpu.make_async_copy(h0_any.at[0, 0], h0, load_sem.at[1])
    load_a = pltpu.make_async_copy(a_any.at[0, 0], a32, load_sem.at[2])
    load_g = [
        pltpu.make_async_copy(g_any.at[0, 0, t], g.at[t], load_sem.at[3 + t])
        for t in range(ticks)
    ]
    load_w.start()
    load_a.start()
    load_h.start()
    for copy in load_g:
        copy.start()

    barrier = pltpu.get_barrier_semaphore()
    for i in range(1, docs):
        pl.semaphore_signal(barrier, inc=1, device_id=(sec, peer(i)), device_id_type=MESH)
    for i in range(1, sections):
        pl.semaphore_signal(
            barrier, inc=1, device_id=(lax.rem(sec + i, sections), me), device_id_type=MESH
        )

    gain_own = gain[:, cols(me, span)].astype(F32)
    keys = w.shape[1]
    gain_col = jnp.broadcast_to(gain_own, (keys, span)).T
    load_w.wait()
    own_w[...] = (w_own[...].astype(F32) * gain_col).astype(BF16)
    pl.semaphore_wait(barrier, docs + sections - 2)

    def w_copy(i):
        return remote(own_w, own_w, send_w.at[i], recv_w.at[me], (sec, peer(i)))

    def w_wait(i):
        p = peer(i)
        block = w.at[pl.ds(pl.multiple_of(p * span, 128), span)]
        remote(block, block, send_w.at[i], recv_w.at[p], (sec, p)).wait_recv()

    for i in range(1, docs):
        w_copy(i).start()

    def tok_copy(t):
        return remote(
            tok_any.at[0, t], hbuf.at[t, pl.ds(0, seg), cols(sec)],
            send_tok.at[t], recv_tok.at[t, sec], (0, me),
        )

    def tok_wait(t, c):
        dst = hbuf.at[t, pl.ds(0, seg), cols(c)]
        pltpu.make_async_copy(tok_any.at[0, t], dst, recv_tok.at[t, c]).wait()

    @pl.when(jnp.logical_not(first))
    def _():
        for t in range(ticks - 1):
            tok_copy(t).start()

    @pl.when(first)
    def _():
        for t in range(ticks - 1):
            dst = hbuf.at[t, pl.ds(0, seg), pl.ds(0, cw)]
            pltpu.make_async_copy(tok_any.at[0, t], dst, recv_tok.at[t, 0]).start()

    def y_whole(t, c):
        return remote(
            ybuf.at[t, :, cols(c)], hbuf.at[t, :, cols(c)],
            send_y.at[t, c], recv_y.at[t, c], (follower, me),
        )

    def y_mem(t, c):
        part = pl.ds(seg, mem)
        return remote(
            ybuf.at[t, part, cols(c)], hbuf.at[t, part, cols(c)],
            send_y.at[t, c], recv_y.at[t, c], (follower, me),
        )

    def forward(t, src, c, owner):
        dst = fbuf.at[t, me, :, cols(lax.rem(c, per))]
        return remote(
            src.at[:, cols(c)], dst, send_f.at[t, c], recv_f.at[t, me, lax.rem(c, per)],
            (sec, owner),
        )

    def k_copy(t, i):
        return remote(
            kbuf.at[t, me], kbuf.at[t, me], send_k.at[t, i], recv_k.at[t, me], (sec, peer(i))
        )

    z[...] = z_in[0]
    load_a.wait()
    load_g[0].wait()

    def first_cot(c, total):
        part = a32[:, cols(c)].astype(BF16)
        a16[:, cols(c)] = part
        return total + dot(g[0, :, cols(c)], part, NT)

    blank = jnp.zeros((rows, keys), F32)
    cot[...] = lax.fori_loop(0, sections, first_cot, blank)
    adt[...] = jnp.zeros_like(adt)
    load_h.wait()
    for i in range(1, docs):
        w_wait(i)

    for t in range(ticks):
        src = h0 if t == 0 else hbuf.at[t - 1]

        def arrive(c, carry, t=t, src=src):
            squares, pre = carry
            if t > 0:
                @pl.when(first)
                def _():
                    tok_wait(t - 1, c)
                    y_mem(t - 1, c).wait_recv()

                @pl.when(jnp.logical_not(first))
                def _():
                    y_whole(t - 1, c).wait_recv()

            owner = lax.div(c, per)

            @pl.when(owner != me)
            def _():
                forward(t, src, c, owner).start()

            h = src[:, cols(c)]
            hf = h.astype(F32)
            for j in range(cw // 128):
                piece = hf[:, j * 128:(j + 1) * 128]
                squares = squares + piece * piece
            return squares, pre + dot(h, w[cols(c), :])

        squares, pre = lax.fori_loop(
            0, sections, arrive, (jnp.zeros((rows, 128), F32), blank)
        )
        scale = lax.rsqrt(jnp.sum(squares, axis=1, keepdims=True) / width + 1e-06)
        pre = pre * scale
        low = jnp.exp(jnp.minimum(pre, 0.0))
        query = jnp.where(pre > 0, pre + 1.0, low)
        zrow = z[...]
        inv = 1.0 / (1.0 + jnp.sum(query * zrow, axis=1, keepdims=True))
        read = (query * inv).astype(BF16)

        def cotangent(t=t, query=query, inv=inv, pre=pre, low=low, scale=scale, zrow=zrow):
            grads = cot[...]
            lean = jnp.sum(query * grads, axis=1, keepdims=True) * inv * inv
            dq = grads * inv - lean * zrow
            kbuf[t, me] = (dq * jnp.where(pre > 0, 1.0, low) * scale).astype(BF16)
            for i in range(1, docs):
                k_copy(t, i).start()

        if t == ticks - 1:
            cotangent()

        def emit(c, carry, t=t, src=src, read=read):
            y = src[:, cols(c)].astype(F32) + dot(read, a16[:, cols(c)])
            if t == ticks - 1:
                y_out[0, 0, :, cols(c)] = y.astype(BF16)
            else:
                ybuf[t, :, cols(c)] = y.astype(BF16)

                @pl.when(last)
                def _():
                    y_mem(t, c).start()

                @pl.when(jnp.logical_not(last))
                def _():
                    y_whole(t, c).start()

            return carry

        lax.fori_loop(0, sections, emit, 0)
        if t < ticks - 1:
            cotangent()
            scale_mem = scale[seg:]

            def values(c, src=src, scale_mem=scale_mem):
                h = src[pl.ds(seg, mem), cols(c)].astype(F32)
                v = h * scale_mem * gain[:, cols(c)].astype(F32)
                return v.astype(BF16).astype(F32)

            def strength(c, total, values=values):
                return total + jnp.sum(
                    values(c) * rate[:, cols(c)].astype(F32), axis=1, keepdims=True
                )

            logit = lax.fori_loop(0, sections, strength, jnp.zeros((mem, 1), F32))
            beta = 1.0 / (1.0 + jnp.exp(-logit))
            mem_query = query[seg:]
            mem_keys = mem_query.astype(BF16)
            mem_read = read[seg:]
            load_g[t + 1].wait()

            def write(c, total, t=t, values=values, beta=beta, mem_keys=mem_keys,
                      mem_read=mem_read):
                prev = dot(mem_read, a16[:, cols(c)])
                delta = (beta * (values(c) - prev)).astype(BF16)
                fresh = a32[:, cols(c)] + dot(mem_keys, delta, TN)
                a32[:, cols(c)] = fresh
                part = fresh.astype(BF16)
                a16[:, cols(c)] = part
                return total + dot(g[t + 1, :, cols(c)], part, NT)

            cot[...] = lax.fori_loop(0, sections, write, blank)
            z[...] = zrow + jnp.sum(mem_query * beta, axis=0, keepdims=True)

        own = src[:, cols(me, span)]
        adt[...] += dot(kbuf[t, me], own, TN)
        for i in range(1, docs):
            p = peer(i)
            for c in range(per):
                dst = fbuf.at[t, p, :, pl.ds(c * cw, cw)]
                remote(
                    dst, dst, send_f.at[t, c], recv_f.at[t, p, c], (sec, p)
                ).wait_recv()
            remote(
                kbuf.at[t, p], kbuf.at[t, p], send_k.at[t, i], recv_k.at[t, p], (sec, p)
            ).wait_recv()
            adt[...] += dot(kbuf[t, p], fbuf[t, p], TN)

    ad_out[0] = (adt[...] * gain_own).T

    for i in range(1, docs):
        w_copy(i).wait_send()
        for t in range(ticks):
            k_copy(t, i).wait_send()

    @pl.when(jnp.logical_not(first))
    def _():
        for t in range(ticks - 1):
            tok_copy(t).wait_send()

    def drain(c, carry):
        for t in range(ticks - 1):
            @pl.when(last)
            def _():
                y_mem(t, c).wait_send()

            @pl.when(jnp.logical_not(last))
            def _():
                y_whole(t, c).wait_send()

        owner = lax.div(c, per)
        for t in range(ticks):
            src = h0 if t == 0 else hbuf.at[t - 1]

            @pl.when(owner != me)
            def _():
                forward(t, src, c, owner).wait_send()

        return carry

    lax.fori_loop(0, sections, drain, 0)


def one_kernel(sections, docs, h0, tok, g, w, gain, rate, store, norm):
    rows, width = h0.shape[2:]
    ticks, seg, keys = g.shape[2], tok.shape[2], w.shape[2]
    span = width // docs
    per = sections // docs
    anywhere = pl.BlockSpec(memory_space=pl.ANY)
    near = pl.BlockSpec(memory_space=pltpu.VMEM)
    dma = pltpu.SemaphoreType.DMA
    return pl.pallas_call(
        functools.partial(fused, sections, docs, ticks, seg),
        out_shape=(
            jax.ShapeDtypeStruct((1, 1, rows, width), BF16),
            jax.ShapeDtypeStruct((1, span, keys), F32),
        ),
        in_specs=[anywhere] * 4 + [near, near, anywhere, near],
        out_specs=(near, near),
        scratch_shapes=[
            pltpu.VMEM((rows, width), BF16),
            pltpu.VMEM((ticks - 1, rows, width), BF16),
            pltpu.VMEM((ticks - 1, rows, width), BF16),
            pltpu.VMEM((ticks, rows, width), BF16),
            pltpu.VMEM((span, keys), BF16),
            pltpu.VMEM((width, keys), BF16),
            pltpu.VMEM((keys, width), F32),
            pltpu.VMEM((keys, width), BF16),
            pltpu.VMEM((1, keys), F32),
            pltpu.VMEM((rows, keys), F32),
            pltpu.VMEM((ticks, docs, rows, span), BF16),
            pltpu.VMEM((ticks, docs, rows, keys), BF16),
            pltpu.VMEM((keys, span), F32),
            dma((3 + ticks,)),
            dma((docs,)), dma((docs,)),
            dma((ticks,)), dma((ticks, sections)),
            dma((ticks, sections)), dma((ticks, sections)),
            dma((ticks, sections)), dma((ticks, docs, per)),
            dma((ticks, docs)), dma((ticks, docs)),
        ],
        compiler_params=pltpu.CompilerParams(
            collective_id=0, has_side_effects=True, vmem_limit_bytes=50 * 2**20
        ),
    )(h0, tok, g, w, gain, rate, store, norm)


def solution(mesh):
    placed = (
        P("dp", "section", None, None),
        P("dp", None, None, "section"),
        P("dp", "section", None, None, None),
        P("section", "dp", None),
        P("section", None),
        P("section", None),
        P("dp", "section", None, None),
        P("dp", "section", None),
    )
    sections, docs = mesh.shape["section"], mesh.shape["dp"]

    def chosen(*args):
        width = args[0].shape[3]
        if sections % docs == 0 and width % (128 * sections) == 0:
            return one_kernel(sections, docs, *args)
        return per_device(*args)

    return jax.shard_map(
        chosen,
        mesh=mesh,
        in_specs=placed,
        out_specs=(P("dp", "section", None, None), P("section", "dp", None)),
        check_vma=False,
    )
```

```python
import functools

import jax
import jax.numpy as jnp
from jax import lax
from jax.experimental import pallas as pl
from jax.experimental.pallas import tpu as pltpu
from jax.sharding import PartitionSpec as P

HIGH = lax.Precision.HIGHEST


def from_behind(array, axis, by):
    peers = lax.axis_size(axis)
    return lax.ppermute(array, axis, [(i, (i + by) % peers) for i in range(peers)])


def per_device(
    initial_block_entries,
    incoming_tokens,
    adjoint_flow,
    address_projector,
    rescale_factor,
    storage_rate_projector,
    associative_store,
    recall_scaling,
):
    leading_block = lax.axis_index("section") == 0
    seg_rows = incoming_tokens.shape[2]
    ticks = adjoint_flow.shape[2]
    line_breadth = initial_block_entries.shape[3]
    keysize = address_projector.shape[2]
    gain_row = rescale_factor[0].astype(jnp.float32)
    beta_col = storage_rate_projector[0]
    value_rows = associative_store[0, 0]
    norm_values = recall_scaling[0, 0]
    whole = lax.all_gather(address_projector[0], "dp", axis=0, tiled=True)
    recurrent_vector = initial_block_entries[0, 0]
    produced_entries = recurrent_vector
    local_total = jnp.zeros((line_breadth, keysize), jnp.float32)
    for tick in range(ticks):
        if tick > 0:
            columns = lax.all_gather(incoming_tokens[0, tick - 1], "section", axis=1, tiled=True)
            shifted_along = from_behind(produced_entries, "section", 1)
            loop_rows = shifted_along[seg_rows:]
            attention_channel = jnp.concatenate([columns, loop_rows], axis=0)
            recurrent_vector = jnp.where(leading_block, attention_channel, shifted_along)
        channel_features = recurrent_vector.astype(jnp.float32)
        meansq = jnp.mean(channel_features * channel_features, axis=-1, keepdims=True)
        normed = (channel_features * lax.rsqrt(meansq + 1e-06) * gain_row).astype(jnp.bfloat16)
        pre = jnp.dot(normed, whole, preferred_element_type=jnp.float32)
        query = jax.nn.elu(pre) + 1.0
        num = jnp.dot(query, value_rows, precision=HIGH)
        den = 1.0 + jnp.dot(query, norm_values, precision=HIGH)
        produced_entries = (channel_features + num / den[:, None]).astype(jnp.bfloat16)
        grad_out = adjoint_flow[0, 0, tick].astype(jnp.float32)
        dnum = grad_out / den[:, None]
        dden = -jnp.sum(grad_out * num, axis=-1) / (den * den)
        dq = (
            jnp.einsum("rd,kd->rk", dnum, value_rows, precision=HIGH)
            + dden[:, None] * norm_values[None, :]
        )
        slope = jnp.where(pre > 0, 1.0, jnp.exp(jnp.minimum(pre, 0.0)))
        key_cot = (dq * slope).astype(jnp.bfloat16)
        term = jnp.einsum("rd,rk->dk", normed, key_cot, preferred_element_type=jnp.float32)
        local_total = local_total + term
        mem_keys = query[seg_rows:]
        mem_vals = normed[seg_rows:].astype(jnp.float32)
        beta = jax.nn.sigmoid(
            jnp.dot(normed[seg_rows:], beta_col, preferred_element_type=jnp.float32)
        )
        prev = jnp.dot(mem_keys, value_rows, precision=HIGH)
        prev = prev / (1.0 + jnp.dot(mem_keys, norm_values, precision=HIGH))[:, None]
        value_rows = value_rows + jnp.einsum(
            "rk,rd->kd", mem_keys, beta[:, None] * (mem_vals - prev), precision=HIGH
        )
        norm_values = norm_values + jnp.einsum("rk,r->k", mem_keys, beta, precision=HIGH)
    summed = lax.psum_scatter(local_total, "dp", scatter_dimension=0, tiled=True)
    return (produced_entries[None, None], summed[None])


MESH = pl.DeviceIdType.MESH
NT = (((1,), (1,)), ((), ()))
TN = (((0,), (0,)), ((), ()))
F32 = jnp.float32
BF16 = jnp.bfloat16


def dot(a, b, dims=(((1,), (0,)), ((), ()))):
    return lax.dot_general(a, b, dims, preferred_element_type=F32)


def fused(
    sections, docs, ticks, seg,
    h0_any, tok_any, g_any, w_any, gain, rate, a_any, z_in,
    y_out, ad_out,
    h0, hbuf, ybuf, g, w_own, w, a32, a16, z, cot, fbuf, kbuf, adt,
    load_sem, send_w, recv_w, send_tok, recv_tok, send_y, recv_y,
    send_f, recv_f, send_k, recv_k,
    head_h, head_a, head_p, send_hh, recv_hh, send_ha, recv_ha, send_hp, recv_hp,
):
    sec, me = lax.axis_index("section"), lax.axis_index("dp")
    rows, width = h0.shape
    mem = rows - seg
    span = width // docs
    cw = width // sections
    per = span // cw
    follower = lax.rem(sec + 1, sections)
    heads = head_h.shape[0]
    first, last = sec == 0, sec == sections - 1

    def peer(i):
        return lax.rem(me + i, docs)

    def cols(c, size=cw):
        return pl.ds(pl.multiple_of(c * size, 128), size)

    def remote(src, dst, send, recv, device):
        return pltpu.make_async_remote_copy(
            src_ref=src, dst_ref=dst, send_sem=send, recv_sem=recv,
            device_id=device, device_id_type=MESH,
        )

    own_w = w.at[pl.ds(pl.multiple_of(me * span, 128), span)]
    load_w = pltpu.make_async_copy(w_any.at[0], w_own, load_sem.at[0])
    load_h = pltpu.make_async_copy(h0_any.at[0, 0], h0, load_sem.at[1])
    load_a = pltpu.make_async_copy(a_any.at[0, 0], a32, load_sem.at[2])
    load_g = [
        pltpu.make_async_copy(g_any.at[0, 0, t], g.at[t], load_sem.at[3 + t])
        for t in range(ticks)
    ]
    load_w.start()
    load_a.start()
    load_h.start()
    for copy in load_g:
        copy.start()

    barrier = pltpu.get_barrier_semaphore()
    for i in range(1, docs):
        pl.semaphore_signal(barrier, inc=1, device_id=(sec, peer(i)), device_id_type=MESH)
    for i in range(1, sections):
        pl.semaphore_signal(
            barrier, inc=1, device_id=(lax.rem(sec + i, sections), me), device_id_type=MESH
        )

    gain_own = gain[:, cols(me, span)].astype(F32)
    keys = w.shape[1]
    gain_col = jnp.broadcast_to(gain_own, (keys, span)).T
    load_w.wait()
    own_w[...] = (w_own[...].astype(F32) * gain_col).astype(BF16)
    pl.semaphore_wait(barrier, docs + sections - 2)

    def w_copy(i):
        return remote(own_w, own_w, send_w.at[i], recv_w.at[me], (sec, peer(i)))

    def w_wait(i):
        p = peer(i)
        block = w.at[pl.ds(pl.multiple_of(p * span, 128), span)]
        remote(block, block, send_w.at[i], recv_w.at[p], (sec, p)).wait_recv()

    for i in range(1, docs):
        w_copy(i).start()

    def tok_copy(t):
        return remote(
            tok_any.at[0, t], hbuf.at[t, pl.ds(0, seg), cols(sec)],
            send_tok.at[t], recv_tok.at[t, sec], (0, me),
        )

    def tok_wait(t, c):
        dst = hbuf.at[t, pl.ds(0, seg), cols(c)]
        pltpu.make_async_copy(tok_any.at[0, t], dst, recv_tok.at[t, c]).wait()

    @pl.when(jnp.logical_not(first))
    def _():
        tok_copy(0).start()

    @pl.when(first)
    def _():
        for t in range(ticks - 1):
            dst = hbuf.at[t, pl.ds(0, seg), pl.ds(0, cw)]
            pltpu.make_async_copy(tok_any.at[0, t], dst, recv_tok.at[t, 0]).start()

    def y_whole(t, c):
        return remote(
            ybuf.at[t, :, cols(c)], hbuf.at[t, :, cols(c)],
            send_y.at[t, c], recv_y.at[t, c], (follower, me),
        )

    def y_mem(t, c):
        part = pl.ds(seg, mem)
        return remote(
            ybuf.at[t, part, cols(c)], hbuf.at[t, part, cols(c)],
            send_y.at[t, c], recv_y.at[t, c], (follower, me),
        )

    def forward(t, src, c, owner):
        dst = fbuf.at[t, me, :, cols(lax.rem(c, per))]
        return remote(
            src.at[:, cols(c)], dst, send_f.at[t, c], recv_f.at[t, me, lax.rem(c, per)],
            (sec, owner),
        )

    def k_copy(t, i):
        return remote(
            kbuf.at[t, me], kbuf.at[t, me], send_k.at[t, i], recv_k.at[t, me], (sec, peer(i))
        )

    def head_copies(c):
        to = (follower, me)
        return (
            remote(h0.at[:, cols(c)], head_h.at[c], send_hh.at[c], recv_hh.at[c], to),
            remote(a16.at[:, cols(c)], head_a.at[c], send_ha.at[c], recv_ha.at[c], to),
        )

    def head_read():
        return remote(head_p.at[0], head_p.at[1], send_hp.at[0], recv_hp.at[0], (follower, me))

    z[...] = z_in[0]
    load_a.wait()

    def narrow(c, carry):
        a16[:, cols(c)] = a32[:, cols(c)].astype(BF16)
        return carry

    lax.fori_loop(0, heads, narrow, 0)
    load_h.wait()

    @pl.when(jnp.logical_not(last))
    def _():
        for c in range(heads):
            for copy in head_copies(c):
                copy.start()

    lax.fori_loop(heads, sections, narrow, 0)
    load_g[0].wait()

    def first_cot(c, total):
        return total + dot(g[0, :, cols(c)], a16[:, cols(c)], NT)

    blank = jnp.zeros((rows, keys), F32)
    cot[...] = lax.fori_loop(0, sections, first_cot, blank)
    adt[...] = jnp.zeros_like(adt)
    for i in range(1, docs):
        w_wait(i)

    for t in range(ticks):
        src = h0 if t == 0 else hbuf.at[t - 1]

        def arrive(c, carry, t=t, src=src):
            squares, pre = carry
            if t > 0:
                @pl.when(first)
                def _():
                    tok_wait(t - 1, c)
                    y_mem(t - 1, c).wait_recv()

                whole = jnp.logical_not(first)
                if t == 1:
                    @pl.when(jnp.logical_and(whole, c < heads))
                    def _():
                        @pl.when(c == 0)
                        def _():
                            head_read().wait_recv()

                        for copy in head_copies(lax.min(c, heads - 1)):
                            copy.wait_recv()
                        at = lax.min(c, heads - 1)
                        y = head_h[at].astype(F32) + dot(head_p[1], head_a[at])
                        hbuf[0, :, cols(c)] = y.astype(BF16)

                    whole = jnp.logical_and(whole, c >= heads)

                @pl.when(whole)
                def _():
                    y_whole(t - 1, c).wait_recv()

            owner = lax.div(c, per)

            @pl.when(owner != me)
            def _():
                forward(t, src, c, owner).start()

            h = src[:, cols(c)]
            hf = h.astype(F32)
            for j in range(cw // 128):
                piece = hf[:, j * 128:(j + 1) * 128]
                squares = squares + piece * piece
            return squares, pre + dot(h, w[cols(c), :])

        squares, pre = lax.fori_loop(
            0, sections, arrive, (jnp.zeros((rows, 128), F32), blank)
        )
        scale = lax.rsqrt(jnp.sum(squares, axis=1, keepdims=True) / width + 1e-06)
        pre = pre * scale
        low = jnp.exp(jnp.minimum(pre, 0.0))
        query = jnp.where(pre > 0, pre + 1.0, low)
        zrow = z[...]
        inv = 1.0 / (1.0 + jnp.sum(query * zrow, axis=1, keepdims=True))
        read = (query * inv).astype(BF16)

        def cotangent(t=t, query=query, inv=inv, pre=pre, low=low, scale=scale, zrow=zrow):
            grads = cot[...]
            lean = jnp.sum(query * grads, axis=1, keepdims=True) * inv * inv
            dq = grads * inv - lean * zrow
            kbuf[t, me] = (dq * jnp.where(pre > 0, 1.0, low) * scale).astype(BF16)
            for i in range(1, docs):
                k_copy(t, i).start()

        if t == 0:
            head_p[0] = read

            @pl.when(jnp.logical_not(last))
            def _():
                head_read().start()

        if t == ticks - 1:
            cotangent()

        def emit(c, carry, t=t, src=src, read=read):
            y = src[:, cols(c)].astype(F32) + dot(read, a16[:, cols(c)])
            if t == ticks - 1:
                y_out[0, 0, :, cols(c)] = y.astype(BF16)
            else:
                ybuf[t, :, cols(c)] = y.astype(BF16)

                @pl.when(last)
                def _():
                    y_mem(t, c).start()

                whole = jnp.logical_not(last)
                if t == 0:
                    whole = jnp.logical_and(whole, c >= heads)

                @pl.when(whole)
                def _():
                    y_whole(t, c).start()

            return carry

        lax.fori_loop(0, sections, emit, 0)
        if 0 < t + 1 < ticks - 1:
            @pl.when(jnp.logical_not(first))
            def _():
                tok_copy(t + 1).start()

        if t < ticks - 1:
            cotangent()
            scale_mem = scale[seg:]

            def values(c, src=src, scale_mem=scale_mem):
                h = src[pl.ds(seg, mem), cols(c)].astype(F32)
                v = h * scale_mem * gain[:, cols(c)].astype(F32)
                return v.astype(BF16).astype(F32)

            def strength(c, total, values=values):
                return total + jnp.sum(
                    values(c) * rate[:, cols(c)].astype(F32), axis=1, keepdims=True
                )

            logit = lax.fori_loop(0, sections, strength, jnp.zeros((mem, 1), F32))
            beta = 1.0 / (1.0 + jnp.exp(-logit))
            mem_query = query[seg:]
            mem_keys = mem_query.astype(BF16)
            mem_read = read[seg:]
            load_g[t + 1].wait()
            if t == 0:
                @pl.when(jnp.logical_not(last))
                def _():
                    head_read().wait_send()
                    for c in range(heads):
                        for copy in head_copies(c):
                            copy.wait_send()

            def write(c, total, t=t, values=values, beta=beta, mem_keys=mem_keys,
                      mem_read=mem_read):
                prev = dot(mem_read, a16[:, cols(c)])
                delta = (beta * (values(c) - prev)).astype(BF16)
                fresh = a32[:, cols(c)] + dot(mem_keys, delta, TN)
                a32[:, cols(c)] = fresh
                part = fresh.astype(BF16)
                a16[:, cols(c)] = part
                return total + dot(g[t + 1, :, cols(c)], part, NT)

            cot[...] = lax.fori_loop(0, sections, write, blank)
            z[...] = zrow + jnp.sum(mem_query * beta, axis=0, keepdims=True)

        own = src[:, cols(me, span)]
        adt[...] += dot(kbuf[t, me], own, TN)
        for i in range(1, docs):
            p = peer(i)
            for c in range(per):
                dst = fbuf.at[t, p, :, pl.ds(c * cw, cw)]
                remote(
                    dst, dst, send_f.at[t, c], recv_f.at[t, p, c], (sec, p)
                ).wait_recv()
            remote(
                kbuf.at[t, p], kbuf.at[t, p], send_k.at[t, i], recv_k.at[t, p], (sec, p)
            ).wait_recv()
            adt[...] += dot(kbuf[t, p], fbuf[t, p], TN)

    ad_out[0] = (adt[...] * gain_own).T

    for i in range(1, docs):
        w_copy(i).wait_send()
        for t in range(ticks):
            k_copy(t, i).wait_send()

    @pl.when(jnp.logical_not(first))
    def _():
        for t in range(ticks - 1):
            tok_copy(t).wait_send()

    def drain(c, carry):
        for t in range(ticks - 1):
            @pl.when(last)
            def _():
                y_mem(t, c).wait_send()

            whole = jnp.logical_not(last)
            if t == 0:
                whole = jnp.logical_and(whole, c >= heads)

            @pl.when(whole)
            def _():
                y_whole(t, c).wait_send()

        owner = lax.div(c, per)
        for t in range(ticks):
            src = h0 if t == 0 else hbuf.at[t - 1]

            @pl.when(owner != me)
            def _():
                forward(t, src, c, owner).wait_send()

        return carry

    lax.fori_loop(0, sections, drain, 0)


def one_kernel(sections, docs, h0, tok, g, w, gain, rate, store, norm):
    rows, width = h0.shape[2:]
    ticks, seg, keys = g.shape[2], tok.shape[2], w.shape[2]
    span = width // docs
    per = sections // docs
    heads = sections // 4
    anywhere = pl.BlockSpec(memory_space=pl.ANY)
    near = pl.BlockSpec(memory_space=pltpu.VMEM)
    dma = pltpu.SemaphoreType.DMA
    return pl.pallas_call(
        functools.partial(fused, sections, docs, ticks, seg),
        out_shape=(
            jax.ShapeDtypeStruct((1, 1, rows, width), BF16),
            jax.ShapeDtypeStruct((1, span, keys), F32),
        ),
        in_specs=[anywhere] * 4 + [near, near, anywhere, near],
        out_specs=(near, near),
        scratch_shapes=[
            pltpu.VMEM((rows, width), BF16),
            pltpu.VMEM((ticks - 1, rows, width), BF16),
            pltpu.VMEM((ticks - 1, rows, width), BF16),
            pltpu.VMEM((ticks, rows, width), BF16),
            pltpu.VMEM((span, keys), BF16),
            pltpu.VMEM((width, keys), BF16),
            pltpu.VMEM((keys, width), F32),
            pltpu.VMEM((keys, width), BF16),
            pltpu.VMEM((1, keys), F32),
            pltpu.VMEM((rows, keys), F32),
            pltpu.VMEM((ticks, docs, rows, span), BF16),
            pltpu.VMEM((ticks, docs, rows, keys), BF16),
            pltpu.VMEM((keys, span), F32),
            dma((3 + ticks,)),
            dma((docs,)), dma((docs,)),
            dma((ticks,)), dma((ticks, sections)),
            dma((ticks, sections)), dma((ticks, sections)),
            dma((ticks, sections)), dma((ticks, docs, per)),
            dma((ticks, docs)), dma((ticks, docs)),
            pltpu.VMEM((heads, rows, width // sections), BF16),
            pltpu.VMEM((heads, keys, width // sections), BF16),
            pltpu.VMEM((2, rows, keys), BF16),
            dma((heads,)), dma((heads,)), dma((heads,)), dma((heads,)), dma((1,)), dma((1,)),
        ],
        compiler_params=pltpu.CompilerParams(
            collective_id=0, has_side_effects=True, vmem_limit_bytes=63 * 2**20
        ),
    )(h0, tok, g, w, gain, rate, store, norm)


def solution(mesh):
    placed = (
        P("dp", "section", None, None),
        P("dp", None, None, "section"),
        P("dp", "section", None, None, None),
        P("section", "dp", None),
        P("section", None),
        P("section", None),
        P("dp", "section", None, None),
        P("dp", "section", None),
    )
    sections, docs = mesh.shape["section"], mesh.shape["dp"]

    def chosen(*args):
        width = args[0].shape[3]
        if sections % docs == 0 and width % (128 * sections) == 0:
            return one_kernel(sections, docs, *args)
        return per_device(*args)

    return jax.shard_map(
        chosen,
        mesh=mesh,
        in_specs=placed,
        out_specs=(P("dp", "section", None, None), P("section", "dp", None)),
        check_vma=False,
    )
```

```python
import functools

import jax
import jax.numpy as jnp
from jax import lax
from jax.experimental import pallas as pl
from jax.experimental.pallas import tpu as pltpu
from jax.sharding import PartitionSpec as P

HIGH = lax.Precision.HIGHEST


def from_behind(array, axis, by):
    peers = lax.axis_size(axis)
    return lax.ppermute(array, axis, [(i, (i + by) % peers) for i in range(peers)])


def per_device(
    initial_block_entries,
    incoming_tokens,
    adjoint_flow,
    address_projector,
    rescale_factor,
    storage_rate_projector,
    associative_store,
    recall_scaling,
):
    leading_block = lax.axis_index("section") == 0
    seg_rows = incoming_tokens.shape[2]
    ticks = adjoint_flow.shape[2]
    line_breadth = initial_block_entries.shape[3]
    keysize = address_projector.shape[2]
    gain_row = rescale_factor[0].astype(jnp.float32)
    beta_col = storage_rate_projector[0]
    value_rows = associative_store[0, 0]
    norm_values = recall_scaling[0, 0]
    whole = lax.all_gather(address_projector[0], "dp", axis=0, tiled=True)
    recurrent_vector = initial_block_entries[0, 0]
    produced_entries = recurrent_vector
    local_total = jnp.zeros((line_breadth, keysize), jnp.float32)
    for tick in range(ticks):
        if tick > 0:
            columns = lax.all_gather(incoming_tokens[0, tick - 1], "section", axis=1, tiled=True)
            shifted_along = from_behind(produced_entries, "section", 1)
            loop_rows = shifted_along[seg_rows:]
            attention_channel = jnp.concatenate([columns, loop_rows], axis=0)
            recurrent_vector = jnp.where(leading_block, attention_channel, shifted_along)
        channel_features = recurrent_vector.astype(jnp.float32)
        meansq = jnp.mean(channel_features * channel_features, axis=-1, keepdims=True)
        normed = (channel_features * lax.rsqrt(meansq + 1e-06) * gain_row).astype(jnp.bfloat16)
        pre = jnp.dot(normed, whole, preferred_element_type=jnp.float32)
        query = jax.nn.elu(pre) + 1.0
        num = jnp.dot(query, value_rows, precision=HIGH)
        den = 1.0 + jnp.dot(query, norm_values, precision=HIGH)
        produced_entries = (channel_features + num / den[:, None]).astype(jnp.bfloat16)
        grad_out = adjoint_flow[0, 0, tick].astype(jnp.float32)
        dnum = grad_out / den[:, None]
        dden = -jnp.sum(grad_out * num, axis=-1) / (den * den)
        dq = (
            jnp.einsum("rd,kd->rk", dnum, value_rows, precision=HIGH)
            + dden[:, None] * norm_values[None, :]
        )
        slope = jnp.where(pre > 0, 1.0, jnp.exp(jnp.minimum(pre, 0.0)))
        key_cot = (dq * slope).astype(jnp.bfloat16)
        term = jnp.einsum("rd,rk->dk", normed, key_cot, preferred_element_type=jnp.float32)
        local_total = local_total + term
        mem_keys = query[seg_rows:]
        mem_vals = normed[seg_rows:].astype(jnp.float32)
        beta = jax.nn.sigmoid(
            jnp.dot(normed[seg_rows:], beta_col, preferred_element_type=jnp.float32)
        )
        prev = jnp.dot(mem_keys, value_rows, precision=HIGH)
        prev = prev / (1.0 + jnp.dot(mem_keys, norm_values, precision=HIGH))[:, None]
        value_rows = value_rows + jnp.einsum(
            "rk,rd->kd", mem_keys, beta[:, None] * (mem_vals - prev), precision=HIGH
        )
        norm_values = norm_values + jnp.einsum("rk,r->k", mem_keys, beta, precision=HIGH)
    summed = lax.psum_scatter(local_total, "dp", scatter_dimension=0, tiled=True)
    return (produced_entries[None, None], summed[None])


MESH = pl.DeviceIdType.MESH
NT = (((1,), (1,)), ((), ()))
TN = (((0,), (0,)), ((), ()))
F32 = jnp.float32
BF16 = jnp.bfloat16


def dot(a, b, dims=(((1,), (0,)), ((), ()))):
    return lax.dot_general(a, b, dims, preferred_element_type=F32)


def fused(
    sections, docs, ticks, seg,
    h0_any, tok_any, g_any, w_any, gain, rate, a_any, z_in,
    y_out, ad_out,
    h0, hbuf, ybuf, g, w_own, w, a32, a16, z, cot, fbuf, kbuf, adt,
    load_sem, send_w, recv_w, send_tok, recv_tok, send_y, recv_y,
    send_f, recv_f, send_k, recv_k,
    head_h, head_a, head_p, send_hh, recv_hh, send_ha, recv_ha, send_hp, recv_hp,
):
    sec, me = lax.axis_index("section"), lax.axis_index("dp")
    rows, width = h0.shape
    mem = rows - seg
    span = width // docs
    cw = width // sections
    per = span // cw
    follower = lax.rem(sec + 1, sections)
    heads = head_h.shape[0]
    first, last = sec == 0, sec == sections - 1

    def peer(i):
        return lax.rem(me + i, docs)

    def cols(c, size=cw):
        return pl.ds(pl.multiple_of(c * size, 128), size)

    def remote(src, dst, send, recv, device):
        return pltpu.make_async_remote_copy(
            src_ref=src, dst_ref=dst, send_sem=send, recv_sem=recv,
            device_id=device, device_id_type=MESH,
        )

    own_w = w.at[pl.ds(pl.multiple_of(me * span, 128), span)]
    load_w = pltpu.make_async_copy(w_any.at[0], w_own, load_sem.at[0])
    load_h = pltpu.make_async_copy(h0_any.at[0, 0], h0, load_sem.at[1])
    load_a = pltpu.make_async_copy(a_any.at[0, 0], a32, load_sem.at[2])
    load_g = [
        pltpu.make_async_copy(g_any.at[0, 0, t], g.at[t], load_sem.at[3 + t])
        for t in range(ticks)
    ]
    load_w.start()
    load_a.start()
    load_h.start()
    for copy in load_g:
        copy.start()

    barrier = pltpu.get_barrier_semaphore()
    for i in range(1, docs):
        pl.semaphore_signal(barrier, inc=1, device_id=(sec, peer(i)), device_id_type=MESH)
    for i in range(1, sections):
        pl.semaphore_signal(
            barrier, inc=1, device_id=(lax.rem(sec + i, sections), me), device_id_type=MESH
        )

    gain_own = gain[:, cols(me, span)].astype(F32)
    keys = w.shape[1]
    gain_col = jnp.broadcast_to(gain_own, (keys, span)).T
    load_w.wait()
    own_w[...] = (w_own[...].astype(F32) * gain_col).astype(BF16)
    pl.semaphore_wait(barrier, docs + sections - 2)

    def w_copy(i):
        return remote(own_w, own_w, send_w.at[i], recv_w.at[me], (sec, peer(i)))

    def w_wait(i):
        p = peer(i)
        block = w.at[pl.ds(pl.multiple_of(p * span, 128), span)]
        remote(block, block, send_w.at[i], recv_w.at[p], (sec, p)).wait_recv()

    for i in range(1, docs):
        w_copy(i).start()

    def tok_copy(t):
        return remote(
            tok_any.at[0, t], hbuf.at[t, pl.ds(0, seg), cols(sec)],
            send_tok.at[t], recv_tok.at[t, sec], (0, me),
        )

    def tok_wait(t, c):
        dst = hbuf.at[t, pl.ds(0, seg), cols(c)]
        pltpu.make_async_copy(tok_any.at[0, t], dst, recv_tok.at[t, c]).wait()

    @pl.when(jnp.logical_not(first))
    def _():
        tok_copy(0).start()

    @pl.when(first)
    def _():
        for t in range(ticks - 1):
            dst = hbuf.at[t, pl.ds(0, seg), pl.ds(0, cw)]
            pltpu.make_async_copy(tok_any.at[0, t], dst, recv_tok.at[t, 0]).start()

    def y_whole(t, c):
        return remote(
            ybuf.at[t, :, cols(c)], hbuf.at[t, :, cols(c)],
            send_y.at[t, c], recv_y.at[t, c], (follower, me),
        )

    def y_mem(t, c):
        part = pl.ds(seg, mem)
        return remote(
            ybuf.at[t, part, cols(c)], hbuf.at[t, part, cols(c)],
            send_y.at[t, c], recv_y.at[t, c], (follower, me),
        )

    def forward(t, src, c, owner):
        dst = fbuf.at[t, me, :, cols(lax.rem(c, per))]
        return remote(
            src.at[:, cols(c)], dst, send_f.at[t, c], recv_f.at[t, me, lax.rem(c, per)],
            (sec, owner),
        )

    def k_copy(t, i):
        return remote(
            kbuf.at[t, me], kbuf.at[t, me], send_k.at[t, i], recv_k.at[t, me], (sec, peer(i))
        )

    def head_copies(c):
        to = (follower, me)
        return (
            remote(h0.at[:, cols(c)], head_h.at[c], send_hh.at[c], recv_hh.at[c], to),
            remote(a16.at[:, cols(c)], head_a.at[c], send_ha.at[c], recv_ha.at[c], to),
        )

    def head_read():
        return remote(head_p.at[0], head_p.at[1], send_hp.at[0], recv_hp.at[0], (follower, me))

    z[...] = z_in[0]
    load_a.wait()

    def narrow(c, carry):
        a16[:, cols(c)] = a32[:, cols(c)].astype(BF16)
        return carry

    lax.fori_loop(0, heads, narrow, 0)
    load_h.wait()

    @pl.when(jnp.logical_not(last))
    def _():
        for c in range(heads):
            for copy in head_copies(c):
                copy.start()

    lax.fori_loop(heads, sections, narrow, 0)
    load_g[0].wait()

    def first_cot(c, total):
        return total + dot(g[0, :, cols(c)], a16[:, cols(c)], NT)

    blank = jnp.zeros((rows, keys), F32)
    cot[...] = lax.fori_loop(0, sections, first_cot, blank)
    adt[...] = jnp.zeros_like(adt)
    for i in range(1, docs):
        w_wait(i)

    def collect(t):
        src = h0 if t == 0 else hbuf.at[t - 1]
        own = src[:, cols(me, span)]
        adt[...] += dot(kbuf[t, me], own, TN)
        for i in range(1, docs):
            p = peer(i)
            for c in range(per):
                dst = fbuf.at[t, p, :, pl.ds(c * cw, cw)]
                remote(
                    dst, dst, send_f.at[t, c], recv_f.at[t, p, c], (sec, p)
                ).wait_recv()
            remote(
                kbuf.at[t, p], kbuf.at[t, p], send_k.at[t, i], recv_k.at[t, p], (sec, p)
            ).wait_recv()
            adt[...] += dot(kbuf[t, p], fbuf[t, p], TN)

    for t in range(ticks):
        src = h0 if t == 0 else hbuf.at[t - 1]

        def arrive(c, carry, t=t, src=src):
            squares, pre = carry
            if t > 0:
                @pl.when(first)
                def _():
                    tok_wait(t - 1, c)
                    y_mem(t - 1, c).wait_recv()

                whole = jnp.logical_not(first)
                if t == 1:
                    @pl.when(jnp.logical_and(whole, c < heads))
                    def _():
                        @pl.when(c == 0)
                        def _():
                            head_read().wait_recv()

                        for copy in head_copies(lax.min(c, heads - 1)):
                            copy.wait_recv()
                        at = lax.min(c, heads - 1)
                        y = head_h[at].astype(F32) + dot(head_p[1], head_a[at])
                        hbuf[0, :, cols(c)] = y.astype(BF16)

                    whole = jnp.logical_and(whole, c >= heads)

                @pl.when(whole)
                def _():
                    y_whole(t - 1, c).wait_recv()

            owner = lax.div(c, per)

            @pl.when(owner != me)
            def _():
                forward(t, src, c, owner).start()

            h = src[:, cols(c)]
            hf = h.astype(F32)
            for j in range(cw // 128):
                piece = hf[:, j * 128:(j + 1) * 128]
                squares = squares + piece * piece
            return squares, pre + dot(h, w[cols(c), :])

        squares, pre = lax.fori_loop(
            0, sections, arrive, (jnp.zeros((rows, 128), F32), blank)
        )
        scale = lax.rsqrt(jnp.sum(squares, axis=1, keepdims=True) / width + 1e-06)
        pre = pre * scale
        low = jnp.exp(jnp.minimum(pre, 0.0))
        query = jnp.where(pre > 0, pre + 1.0, low)
        zrow = z[...]
        inv = 1.0 / (1.0 + jnp.sum(query * zrow, axis=1, keepdims=True))
        read = (query * inv).astype(BF16)

        def cotangent(t=t, query=query, inv=inv, pre=pre, low=low, scale=scale, zrow=zrow):
            grads = cot[...]
            lean = jnp.sum(query * grads, axis=1, keepdims=True) * inv * inv
            dq = grads * inv - lean * zrow
            kbuf[t, me] = (dq * jnp.where(pre > 0, 1.0, low) * scale).astype(BF16)
            for i in range(1, docs):
                k_copy(t, i).start()

        if t == 0:
            head_p[0] = read

            @pl.when(jnp.logical_not(last))
            def _():
                head_read().start()

        if t == ticks - 1:
            cotangent()

        def emit(c, carry, t=t, src=src, read=read):
            y = src[:, cols(c)].astype(F32) + dot(read, a16[:, cols(c)])
            if t == ticks - 1:
                y_out[0, 0, :, cols(c)] = y.astype(BF16)
            else:
                ybuf[t, :, cols(c)] = y.astype(BF16)

                @pl.when(last)
                def _():
                    y_mem(t, c).start()

                whole = jnp.logical_not(last)
                if t == 0:
                    whole = jnp.logical_and(whole, c >= heads)

                @pl.when(whole)
                def _():
                    y_whole(t, c).start()

            return carry

        lax.fori_loop(0, sections, emit, 0, unroll=4 if t == ticks - 1 else 1)
        if 0 < t + 1 < ticks - 1:
            @pl.when(jnp.logical_not(first))
            def _():
                tok_copy(t + 1).start()

        if t < ticks - 1:
            cotangent()
            scale_mem = scale[seg:]

            def values(c, src=src, scale_mem=scale_mem):
                h = src[pl.ds(seg, mem), cols(c)].astype(F32)
                v = h * scale_mem * gain[:, cols(c)].astype(F32)
                return v.astype(BF16).astype(F32)

            def strength(c, total, values=values):
                return total + jnp.sum(
                    values(c) * rate[:, cols(c)].astype(F32), axis=1, keepdims=True
                )

            logit = lax.fori_loop(0, sections, strength, jnp.zeros((mem, 1), F32))
            beta = 1.0 / (1.0 + jnp.exp(-logit))
            mem_query = query[seg:]
            mem_keys = mem_query.astype(BF16)
            mem_read = read[seg:]
            load_g[t + 1].wait()
            if t == 0:
                @pl.when(jnp.logical_not(last))
                def _():
                    head_read().wait_send()
                    for c in range(heads):
                        for copy in head_copies(c):
                            copy.wait_send()

            def write(c, total, t=t, values=values, beta=beta, mem_keys=mem_keys,
                      mem_read=mem_read):
                prev = dot(mem_read, a16[:, cols(c)])
                delta = (beta * (values(c) - prev)).astype(BF16)
                fresh = a32[:, cols(c)] + dot(mem_keys, delta, TN)
                a32[:, cols(c)] = fresh
                part = fresh.astype(BF16)
                a16[:, cols(c)] = part
                return total + dot(g[t + 1, :, cols(c)], part, NT)

            cot[...] = lax.fori_loop(0, sections, write, blank)
            z[...] = zrow + jnp.sum(mem_query * beta, axis=0, keepdims=True)

        if 0 < t < ticks - 1:
            collect(t - 1)
        if t >= ticks - 2:
            collect(t)

    ad_out[0] = (adt[...] * gain_own).T

    for i in range(1, docs):
        w_copy(i).wait_send()
        for t in range(ticks):
            k_copy(t, i).wait_send()

    @pl.when(jnp.logical_not(first))
    def _():
        for t in range(ticks - 1):
            tok_copy(t).wait_send()

    def drain(c, carry):
        for t in range(ticks - 1):
            @pl.when(last)
            def _():
                y_mem(t, c).wait_send()

            whole = jnp.logical_not(last)
            if t == 0:
                whole = jnp.logical_and(whole, c >= heads)

            @pl.when(whole)
            def _():
                y_whole(t, c).wait_send()

        owner = lax.div(c, per)
        for t in range(ticks):
            src = h0 if t == 0 else hbuf.at[t - 1]

            @pl.when(owner != me)
            def _():
                forward(t, src, c, owner).wait_send()

        return carry

    lax.fori_loop(0, sections, drain, 0)


def one_kernel(sections, docs, h0, tok, g, w, gain, rate, store, norm):
    rows, width = h0.shape[2:]
    ticks, seg, keys = g.shape[2], tok.shape[2], w.shape[2]
    span = width // docs
    per = sections // docs
    heads = sections // 4
    anywhere = pl.BlockSpec(memory_space=pl.ANY)
    near = pl.BlockSpec(memory_space=pltpu.VMEM)
    dma = pltpu.SemaphoreType.DMA
    return pl.pallas_call(
        functools.partial(fused, sections, docs, ticks, seg),
        out_shape=(
            jax.ShapeDtypeStruct((1, 1, rows, width), BF16),
            jax.ShapeDtypeStruct((1, span, keys), F32),
        ),
        in_specs=[anywhere] * 4 + [near, near, anywhere, near],
        out_specs=(near, near),
        scratch_shapes=[
            pltpu.VMEM((rows, width), BF16),
            pltpu.VMEM((ticks - 1, rows, width), BF16),
            pltpu.VMEM((ticks - 1, rows, width), BF16),
            pltpu.VMEM((ticks, rows, width), BF16),
            pltpu.VMEM((span, keys), BF16),
            pltpu.VMEM((width, keys), BF16),
            pltpu.VMEM((keys, width), F32),
            pltpu.VMEM((keys, width), BF16),
            pltpu.VMEM((1, keys), F32),
            pltpu.VMEM((rows, keys), F32),
            pltpu.VMEM((ticks, docs, rows, span), BF16),
            pltpu.VMEM((ticks, docs, rows, keys), BF16),
            pltpu.VMEM((keys, span), F32),
            dma((3 + ticks,)),
            dma((docs,)), dma((docs,)),
            dma((ticks,)), dma((ticks, sections)),
            dma((ticks, sections)), dma((ticks, sections)),
            dma((ticks, sections)), dma((ticks, docs, per)),
            dma((ticks, docs)), dma((ticks, docs)),
            pltpu.VMEM((heads, rows, width // sections), BF16),
            pltpu.VMEM((heads, keys, width // sections), BF16),
            pltpu.VMEM((2, rows, keys), BF16),
            dma((heads,)), dma((heads,)), dma((heads,)), dma((heads,)), dma((1,)), dma((1,)),
        ],
        compiler_params=pltpu.CompilerParams(
            collective_id=0, has_side_effects=True, vmem_limit_bytes=63 * 2**20
        ),
    )(h0, tok, g, w, gain, rate, store, norm)


def solution(mesh):
    placed = (
        P("dp", "section", None, None),
        P("dp", None, None, "section"),
        P("dp", "section", None, None, None),
        P("section", "dp", None),
        P("section", None),
        P("section", None),
        P("dp", "section", None, None),
        P("dp", "section", None),
    )
    sections, docs = mesh.shape["section"], mesh.shape["dp"]

    def chosen(*args):
        width = args[0].shape[3]
        if sections % docs == 0 and width % (128 * sections) == 0:
            return one_kernel(sections, docs, *args)
        return per_device(*args)

    return jax.shard_map(
        chosen,
        mesh=mesh,
        in_specs=placed,
        out_specs=(P("dp", "section", None, None), P("section", "dp", None)),
        check_vma=False,
    )
```
